768 devices in a mesh: section: 4 (over y_lo), fsdp: 192 (over x, y_hi, z, core).
Axes of the slice: x: 4, y: 8 (y_hi: 2, y_lo: 4; y = y_hi * 4 + y_lo), z: 12, core: 2. Of those that a mesh axis runs over, the one named last changes fastest.
Arguments:
- hidden: bfloat16 [4, 24576, 4608], P('section', 'fsdp'), may hold values from -24 to 24
- gain: bfloat16 [4, 4608], P('section'), may hold values from 0.099609375 to 1.8984375
- key_grad: bfloat16 [4, 24576, 512], P('section', 'fsdp'), may hold values from -6 to 6
- residual_grad: bfloat16 [4, 24576, 4608], P('section', 'fsdp'), may hold values from -6 to 6
- key_weight: bfloat16 [4, 4608, 512], P('section', 'fsdp'), may hold values from -0.09375 to 0.09375
Outputs:
- passed_grad: bfloat16 [4, 24576, 4608], P('section', 'fsdp')
- weight_grad: float32 [4, 4608, 512], P('section', 'fsdp')
The draws below stay inside these ranges and needn't reach their ends.
All inputs are finite; a program needn't handle non-finite values.
Results may differ from the reference program's by a relative error of at most 0.0029.
Values may be sent and summed in bfloat16 or wider, within the bound.
A program may use at most 64 MiB of HBM per device.

```python
import math
import jax
import jax.numpy as jnp
from jax import lax

D = 4608
KW = 512
TOKENS = 24576
SECTIONS = 4


def with_spikes(array, rng, source, target, shards_of, factor):
    def block_of(position):
        return (jnp.arange(array.shape[position]) // (array.shape[position] // shards_of)).reshape((-1,) + (1,) * (array.ndim - 1 - position))

    near = jax.random.permutation(rng, shards_of)[block_of(target)]
    far = (block_of(target) + shards_of // 2) % shards_of
    return jnp.where((block_of(source) == near) | (block_of(source) == far), factor * array, array)


def block_scale(stream_key, extent, shards, smallest, largest):
    factor_of = 1.0
    for position, parts in shards:
        draws = jax.random.uniform(jax.random.fold_in(jax.random.fold_in(stream_key, 6), position), (parts,), jnp.float32, smallest / len(shards), largest / len(shards))
        factor_of = factor_of * jnp.repeat(jnp.exp(draws), extent[position] // parts).reshape((-1,) + (1,) * (len(extent) - 1 - position))
    return factor_of


def centred(rng, extent, width, bound, shards=(), kind=jnp.bfloat16):
    result = jax.random.normal(rng, extent, jnp.float32) * width
    if len(shards) > 0:
        result = block_scale(rng, extent, shards, -0.22, 0.18) * result
    return jnp.clip(result, min=-bound, max=bound).astype(kind)


def gaussian_with(key, dims, deviation, bound, split, heavy, held_as=jnp.bfloat16):
    drawn = deviation * jax.random.normal(key, dims, jnp.float32)
    if split:
        drawn = drawn * block_scale(key, dims, split, -0.22, 0.18)
    return jnp.clip(with_spikes(drawn, jax.random.fold_in(key, 3), *heavy), -bound, bound).astype(held_as)


def setup_inputs(seed: int = 0) -> dict:
    arg_keys = jax.random.split(jax.random.key(seed), 6)
    hidden = gaussian_with(arg_keys[0], (SECTIONS, TOKENS, D), 1.0, 24.0, ((0, 4), (1, 192)), (1, 2, 192, 6.0))
    gain = jnp.clip(1.0 + 0.18 * jax.random.normal(arg_keys[1], (SECTIONS, D), jnp.float32), 0.099609375, 1.8984375).astype(jnp.bfloat16)
    key_grad = centred(arg_keys[2], (SECTIONS, TOKENS, KW), 1.0, 6.0, ((0, 4), (1, 192)))
    residual_grad = centred(arg_keys[3], (SECTIONS, TOKENS, D), 0.5, 6.0, ((0, 4), (1, 192)))
    key_weight = centred(arg_keys[4], (SECTIONS, D, KW), D ** -0.5, 0.09375, ((0, 4), (1, 192)))
    return dict(hidden=hidden, gain=gain, key_grad=key_grad, residual_grad=residual_grad, key_weight=key_weight)


def one_section(hidden, gain, key_grad, residual_grad, key_weight):
    x = hidden.astype(jnp.float32)
    g = gain.astype(jnp.float32)
    scale = 1.0 / jnp.sqrt(lax.optimization_barrier(jnp.mean(x * x, axis=-1, keepdims=True)) + 1e-05)
    normed = (x * scale * g).astype(jnp.bfloat16)
    grad_w = lax.dot_general(normed, key_grad, (((0,), (0,)), ((), ())), preferred_element_type=jnp.float32)
    grad_w = grad_w / math.sqrt(TOKENS)
    normed_grad = lax.dot_general(key_grad, key_weight, (((1,), (1,)), ((), ())), preferred_element_type=jnp.float32)
    weighted = normed_grad * g
    inner = lax.optimization_barrier(jnp.mean(weighted * x, axis=-1, keepdims=True))
    input_grad = weighted * scale - x * inner * scale * scale * scale + residual_grad.astype(jnp.float32)
    return (input_grad.astype(jnp.bfloat16), grad_w)

def reference(hidden, gain, key_grad, residual_grad, key_weight):
    inputs = []
    weights = []
    for section_id in range(SECTIONS):
        got, grad_w = one_section(hidden[section_id], gain[section_id], key_grad[section_id], residual_grad[section_id], key_weight[section_id])
        inputs.append(got)
        weights.append(grad_w)
    passed = inputs[1:] + [jnp.zeros_like(inputs[0])]
    return (jnp.stack(passed), jnp.stack(weights))
```

```python
import functools
import math

import jax
import jax.numpy as jnp
from jax import lax
from jax.experimental import pallas as pl
from jax.experimental.pallas import tpu as pltpu
from jax.sharding import PartitionSpec as P

MESH = pl.DeviceIdType.MESH
NX, NY, NZ, NS = 4, 2, 12, 4
RIGHT, LEFT = NZ // 2, (NZ - 1) // 2
TOK, KW, ROWS = 128, 512, 24
HALF = KW // 2
COLS = NY * NZ * 2 * ROWS
D = NX * COLS
TILE = 384
TILES = COLS // TILE
PAIRS = TILE // (2 * ROWS)
CHUNK = 16
CHUNKS = TOK // CHUNK
LAG = 1


def kernel(
    total_tokens,
    hidden,
    gain,
    key_grad,
    residual,
    key_weight,
    passed,
    grad_w,
    hid,
    res,
    grads,
    gains,
    scales,
    zeros,
    pair,
    weight,
    normed_out,
    normed_in,
    grads_in,
    part,
    part_in,
    land,
    across,
    normed_grad,
    result,
    load_sem,
    pair_sem,
    y_sem,
    x_send,
    x_recv,
    z_send,
    z_recv,
    share_send,
    share_recv,
    grads_send,
    grads_recv,
    normed_send,
    normed_recv,
    part_send,
    part_recv,
    sum_send,
    sum_recv,
    across_sem,
    pass_send,
    pass_recv,
):
    s = lax.axis_index("section")
    f = lax.axis_index("fsdp")
    core = lax.rem(f, 2)
    z = lax.rem(f // 2, NZ)
    y = lax.rem(f // (2 * NZ), NY)
    x = f // (2 * NZ * NY)

    def at(x_, y_, z_, core_):
        return (s, ((x_ * NY + y_) * NZ + z_) * 2 + core_)

    def shift_z(by):
        return lax.rem(z + (by + 2 * NZ), NZ)

    sibling = at(x, y, z, 1 - core)
    mirror = at(x, 1 - y, z, core)
    right = at(x, y, shift_z(1), core)
    left = at(x, y, shift_z(-1), core)
    others = [at(lax.rem(x + k, NX), y, z, core) for k in range(1, NX)]
    before, after = (s - 1, f), (s + 1, f)

    def remote(src, dst, send, recv, device):
        copy = pltpu.make_async_remote_copy(
            src_ref=src,
            dst_ref=dst,
            send_sem=send,
            recv_sem=recv,
            device_id=device,
            device_id_type=MESH,
        )
        return copy

    load_hidden = pltpu.make_async_copy(hidden.at[0], hid, load_sem.at[0])
    load_grads = pltpu.make_async_copy(key_grad.at[0], grads, load_sem.at[1])
    load_residual = pltpu.make_async_copy(residual.at[0], res, load_sem.at[2])
    load_hidden.start()
    load_grads.start()
    load_residual.start()

    barrier = pltpu.get_barrier_semaphore()
    for device in [sibling, mirror, right, left] + others:
        pl.semaphore_signal(barrier, 1, device_id=device, device_id_type=MESH)

    @pl.when(s < NS - 1)
    def _():
        pl.semaphore_signal(barrier, 1, device_id=after, device_id_type=MESH)

    pair[core] = key_weight[0].astype(jnp.float32)
    gains[...] = gain[...].astype(jnp.float32)
    pl.semaphore_wait(barrier, 4 + len(others) + jnp.minimum(s, 1))

    sent = []

    def start(copy):
        copy.start()
        sent.append(copy)
        return copy

    swap = start(remote(pair.at[core], pair.at[core], pair_sem.at[0], pair_sem.at[1], sibling))
    swap.wait_recv()
    block = pair[...].reshape(2 * ROWS, KW)
    weight[core, x, y, z] = jnp.where(core == 0, block[:, :HALF], block[:, HALF:]).astype(jnp.bfloat16)

    def own(plane):
        return weight.at[core, x, plane, z]

    def spread_x(plane, index):
        return [
            start(remote(own(plane), own(plane), x_send.at[index, k], x_recv.at[index, k], others[k]))
            for k in range(NX - 1)
        ]

    planes = [y, 1 - y]
    to_mirror = start(remote(own(y), own(y), y_sem.at[0], y_sem.at[1], mirror))
    x_copies = [spread_x(y, 0), None]

    load_grads.wait()
    grads_copies = [
        start(remote(grads, grads_in.at[x], grads_send.at[k], grads_recv.at[k], others[k]))
        for k in range(NX - 1)
    ]
    grads_in[x] = grads[...]

    load_hidden.wait()

    @pl.loop(0, CHUNKS)
    def _(c):
        rows = pl.ds(pl.multiple_of(c * CHUNK, CHUNK), CHUNK)
        total = jnp.zeros((CHUNK, 1), jnp.float32)
        for j in range(NX):
            h = hid[rows, pl.ds(j * COLS, COLS)].astype(jnp.float32)
            total += jnp.sum(h * h, axis=-1, keepdims=True)
        scale = 1.0 / jnp.sqrt(total / D + 1e-05)
        scales[rows, :] = jnp.broadcast_to(scale, (CHUNK, 128))
        for j in range(NX):
            h = hid[rows, pl.ds(j * COLS, COLS)].astype(jnp.float32)
            normed = h * scale * gains[:, pl.ds(j * COLS, COLS)]
            normed_out[j, rows, :] = normed.astype(jnp.bfloat16)

    def spread_normed():
        copies = []
        for k in range(NX - 1):
            to = lax.rem(x + k + 1, NX)
            copies.append(
                start(
                    remote(normed_out.at[to], normed_in.at[x], normed_send.at[k], normed_recv.at[k], others[k])
                )
            )
        normed_in[x] = normed_out[x]
        return copies

    def slot(index, by):
        return weight.at[core, :, planes[index], shift_z(by)]

    def share(index, by, order):
        return start(
            remote(slot(index, by), slot(index, by), share_send.at[index, order], share_recv.at[index, order], sibling)
        )

    shares, ring = [], {}

    def ring_step(index, step):
        if step == 0:
            if index == 1:
                to_mirror.wait_recv()
                x_copies[1] = spread_x(planes[1], 1)
            for copy in x_copies[index]:
                copy.wait_recv()
        for way, (device, steps, sign) in enumerate(((right, RIGHT, -1), (left, LEFT, 1))):
            if 0 < step <= steps:
                ring[way, index, step - 1].wait_recv()
            if step < steps:
                ring[way, index, step] = start(
                    remote(
                        slot(index, sign * step),
                        slot(index, sign * step),
                        z_send.at[way, index, step],
                        z_recv.at[way, index, step],
                        device,
                    )
                )
            if step == 0 and way == 0:
                shares.append(share(index, 0, 0))
            if 0 < step <= steps:
                shares.append(share(index, sign * step, step if way == 0 else RIGHT + step))

    def part_tile(t):
        lhs = normed_in[:, :, pl.ds(t * TILE, TILE)].reshape(NX * TOK, TILE)
        product = lax.dot_general(
            lhs,
            grads_in[...].reshape(NX * TOK, KW),
            (((0,), (0,)), ((), ())),
            preferred_element_type=jnp.float32,
        )
        part[pl.ds(t * PAIRS, PAIRS)] = product.reshape(PAIRS, 2, ROWS, KW)
        return start(
            remote(
                part.at[pl.ds(t * PAIRS, PAIRS), 1 - core],
                part_in.at[pl.ds(t * PAIRS, PAIRS)],
                part_send.at[t],
                part_recv.at[t],
                sibling,
            )
        )

    part_copies = []
    for turn in range(RIGHT + LAG + 1):
        if turn <= RIGHT:
            ring_step(0, turn)
        if turn == 0:
            normed_copies = spread_normed()
        if turn == RIGHT - 1:
            for copy in grads_copies + normed_copies:
                copy.wait_recv()
        if RIGHT - 1 <= turn < RIGHT - 1 + TILES and turn <= RIGHT + LAG:
            part_copies.append(part_tile(turn - RIGHT + 1))
        if turn >= LAG:
            ring_step(1, turn - LAG)
    for t in range(len(part_copies), TILES):
        part_copies.append(part_tile(t))
    for copy in part_copies:
        copy.wait_recv()

    sums = {}

    def sum_step(step):
        for way, (device, steps, sign) in enumerate(((right, RIGHT, 1), (left, LEFT, -1))):
            if step >= steps:
                continue
            for half in range(NY):
                pair_index = half * NZ + shift_z(sign * (steps - step))
                value = part[pair_index, core] + part_in[pair_index]
                if step > 0:
                    sums[way, half, step - 1].wait_recv()
                    value += land[way, step - 1, half]
                part[pair_index, core] = value
                sums[way, half, step] = start(
                    remote(
                        part.at[pair_index, core],
                        land.at[way, step, half],
                        sum_send.at[way, step, half],
                        sum_recv.at[way, step, half],
                        device,
                    )
                )

    sum_step(0)
    for copy in shares:
        copy.wait_recv()

    @pl.loop(0, NX)
    def _(j):
        total = None
        for half in range(2):
            term = lax.dot_general(
                grads[:, pl.ds(half * HALF, HALF)],
                weight[half, j].reshape(COLS, HALF),
                (((1,), (1,)), ((), ())),
                preferred_element_type=jnp.float32,
            )
            total = term if total is None else total + term
        normed_grad[j] = total

    load_residual.wait()
    passes = []
    for c in range(CHUNKS):
        passes.append(
            remote(
                result.at[pl.ds(c * CHUNK, CHUNK)],
                passed.at[0, pl.ds(c * CHUNK, CHUNK)],
                pass_send.at[c],
                pass_recv.at[c],
                before,
            )
        )

    def input_grad(c):
        rows = pl.ds(c * CHUNK, CHUNK)
        scale = scales[rows, 0:1]
        total = jnp.zeros((CHUNK, 1), jnp.float32)
        for j in range(NX):
            cols = pl.ds(j * COLS, COLS)
            h = hid[rows, cols].astype(jnp.float32)
            weighted = normed_grad[j, rows, :] * gains[:, cols]
            total += jnp.sum(weighted * h, axis=-1, keepdims=True)
        factor = total / D * scale * scale * scale
        for j in range(NX):
            cols = pl.ds(j * COLS, COLS)
            h = hid[rows, cols].astype(jnp.float32)
            weighted = normed_grad[j, rows, :] * gains[:, cols]
            value = weighted * scale - h * factor + res[rows, cols].astype(jnp.float32)
            result[rows, cols] = value.astype(jnp.bfloat16)
        passes[c].start()

    @pl.when(s > 0)
    def _():
        for c in range(CHUNKS):
            input_grad(c)

    blanks = [
        pltpu.make_async_copy(zeros, passed.at[0, pl.ds(c * CHUNK, CHUNK)], pass_recv.at[c])
        for c in range(CHUNKS)
    ]

    @pl.when(s == NS - 1)
    def _():
        zeros[...] = jnp.zeros_like(zeros)
        for copy in blanks:
            copy.start()

    for step in range(1, RIGHT):
        sum_step(step)

    totals = []
    for half in range(NY):
        pair_index = half * NZ + z
        sums[0, half, RIGHT - 1].wait_recv()
        sums[1, half, LEFT - 1].wait_recv()
        value = part[pair_index, core] + part_in[pair_index]
        value += land[0, RIGHT - 1, half] + land[1, LEFT - 1, half]
        part[pair_index, core] = value
    over = start(
        remote(part.at[(1 - y) * NZ + z, core], across, across_sem.at[0], across_sem.at[1], mirror)
    )
    over.wait_recv()
    grad_w[0] = (part[y * NZ + z, core] + across[...]) / math.sqrt(total_tokens)

    @pl.when(s < NS - 1)
    def _():
        for copy in passes:
            copy.wait_recv()

    @pl.when(s == NS - 1)
    def _():
        for copy in blanks:
            copy.wait()

    for copy in sent:
        copy.wait_send()

    @pl.when(s > 0)
    def _():
        for copy in passes:
            copy.wait_send()


def body(hidden, gain, key_grad, residual_grad, key_weight):
    total_tokens = hidden.shape[1] * lax.axis_size("fsdp")
    bf16, f32 = jnp.bfloat16, jnp.float32
    dma = pltpu.SemaphoreType.DMA
    return pl.pallas_call(
        functools.partial(kernel, total_tokens),
        out_shape=(
            jax.ShapeDtypeStruct((1, TOK, D), bf16),
            jax.ShapeDtypeStruct((1, ROWS, KW), f32),
        ),
        in_specs=[
            pl.BlockSpec(memory_space=pl.ANY),
            pl.BlockSpec(memory_space=pltpu.VMEM),
            pl.BlockSpec(memory_space=pl.ANY),
            pl.BlockSpec(memory_space=pl.ANY),
            pl.BlockSpec(memory_space=pltpu.VMEM),
        ],
        out_specs=(
            pl.BlockSpec(memory_space=pl.ANY),
            pl.BlockSpec(memory_space=pltpu.VMEM),
        ),
        scratch_shapes=[
            pltpu.VMEM((TOK, D), bf16),
            pltpu.VMEM((TOK, D), bf16),
            pltpu.VMEM((TOK, KW), bf16),
            pltpu.VMEM((1, D), f32),
            pltpu.VMEM((TOK, 128), f32),
            pltpu.VMEM((CHUNK, D), bf16),
            pltpu.VMEM((2, ROWS, KW), f32),
            pltpu.VMEM((2, NX, NY, NZ, 2 * ROWS, HALF), bf16),
            pltpu.VMEM((NX, TOK, COLS), bf16),
            pltpu.VMEM((NX, TOK, COLS), bf16),
            pltpu.VMEM((NX, TOK, KW), bf16),
            pltpu.VMEM((NY * NZ, 2, ROWS, KW), f32),
            pltpu.VMEM((NY * NZ, ROWS, KW), f32),
            pltpu.VMEM((2, RIGHT, NY, ROWS, KW), f32),
            pltpu.VMEM((ROWS, KW), f32),
            pltpu.VMEM((NX, TOK, COLS), f32),
            pltpu.VMEM((TOK, D), bf16),
            dma((3,)),
            dma((2,)),
            dma((2,)),
            dma((2, NX - 1)),
            dma((2, NX - 1)),
            dma((2, 2, RIGHT)),
            dma((2, 2, RIGHT)),
            dma((2, NZ)),
            dma((2, NZ)),
            dma((NX - 1,)),
            dma((NX - 1,)),
            dma((NX - 1,)),
            dma((NX - 1,)),
            dma((TILES,)),
            dma((TILES,)),
            dma((2, RIGHT, NY)),
            dma((2, RIGHT, NY)),
            dma((2,)),
            dma((CHUNKS,)),
            dma((CHUNKS,)),
        ],
        compiler_params=pltpu.CompilerParams(
            collective_id=0, has_side_effects=True, vmem_limit_bytes=60 * 2**20
        ),
        cost_estimate=pl.CostEstimate(
            flops=4 * TOK * D * KW, bytes_accessed=16 * 2**20, transcendentals=TOK
        ),
        name="key_backward",
    )(hidden, gain, key_grad, residual_grad, key_weight)


def solution(mesh):
    return jax.shard_map(
        body,
        mesh=mesh,
        in_specs=(
            P("section", "fsdp", None),
            P("section", None),
            P("section", "fsdp", None),
            P("section", "fsdp", None),
            P("section", "fsdp", None),
        ),
        out_specs=(P("section", "fsdp", None), P("section", "fsdp", None)),
        check_vma=False,
    )
```

```python
import functools
import math

import jax
import jax.numpy as jnp
from jax import lax
from jax.experimental import pallas as pl
from jax.experimental.pallas import tpu as pltpu
from jax.sharding import PartitionSpec as P

MESH = pl.DeviceIdType.MESH
NX, NY, NZ, NS = 4, 2, 12, 4
RIGHT, LEFT = NZ // 2, (NZ - 1) // 2
TOK, KW, ROWS = 128, 512, 24
QUARTER = KW // 4
PIECES, PIECE = 2, KW // 2
COLS = NY * NZ * 2 * ROWS
D = NX * COLS
TILE = 384
TILES = COLS // TILE
PAIRS = TILE // (2 * ROWS)
CHUNK = 16
CHUNKS = TOK // CHUNK
LAG = 1
SEND_NORMED = 2


def kernel(
    total_tokens,
    hidden,
    gain,
    key_grad,
    residual,
    key_weight,
    passed,
    grad_w,
    hid,
    res,
    gain_in,
    weight_in,
    grads,
    gains,
    scales,
    zeros,
    pair,
    weight,
    normed_out,
    normed_in,
    grads_in,
    part,
    part_in,
    land,
    across,
    normed_grad,
    result,
    load_sem,
    pair_sem,
    y_sem,
    x_send,
    x_recv,
    z_send,
    z_recv,
    share_send,
    share_recv,
    late_send,
    late_recv,
    grads_send,
    grads_recv,
    normed_send,
    normed_recv,
    part_send,
    part_recv,
    sum_send,
    sum_recv,
    across_send,
    across_recv,
    pass_send,
    pass_recv,
):
    s = lax.axis_index("section")
    f = lax.axis_index("fsdp")
    core = lax.rem(f, 2)
    z = lax.rem(f // 2, NZ)
    y = lax.rem(f // (2 * NZ), NY)
    x = f // (2 * NZ * NY)

    def at(x_, y_, z_, core_):
        return (s, ((x_ * NY + y_) * NZ + z_) * 2 + core_)

    def shift_z(by):
        return lax.rem(z + (by + 2 * NZ), NZ)

    sibling = at(x, y, z, 1 - core)
    mirror = at(x, 1 - y, z, core)
    right = at(x, y, shift_z(1), core)
    left = at(x, y, shift_z(-1), core)
    others = [at(lax.rem(x + k, NX), y, z, core) for k in range(1, NX)]
    before, after = (s - 1, f), (s + 1, f)

    def remote(src, dst, send, recv, device):
        copy = pltpu.make_async_remote_copy(
            src_ref=src,
            dst_ref=dst,
            send_sem=send,
            recv_sem=recv,
            device_id=device,
            device_id_type=MESH,
        )
        return copy

    load_hidden = pltpu.make_async_copy(hidden.at[0], hid, load_sem.at[0])
    load_grads = pltpu.make_async_copy(key_grad.at[0], grads, load_sem.at[1])
    load_residual = pltpu.make_async_copy(residual.at[0], res, load_sem.at[2])
    load_hidden.start()
    load_grads.start()
    load_residual.start()
    load_gain = pltpu.make_async_copy(gain, gain_in, load_sem.at[3])
    load_weight = pltpu.make_async_copy(key_weight, weight_in, load_sem.at[4])
    load_gain.start()
    load_weight.start()

    barrier = pltpu.get_barrier_semaphore()
    for device in [sibling, mirror, right, left] + others:
        pl.semaphore_signal(barrier, 1, device_id=device, device_id_type=MESH)

    @pl.when(s < NS - 1)
    def _():
        pl.semaphore_signal(barrier, 1, device_id=after, device_id_type=MESH)

    load_weight.wait()
    pair[core] = weight_in[0].astype(jnp.float32)
    load_gain.wait()
    gains[...] = gain_in[...].astype(jnp.float32)
    pl.semaphore_wait(barrier, 4 + len(others) + jnp.minimum(s, 1))

    sent = []

    def start(copy):
        copy.start()
        sent.append(copy)
        return copy

    swap = start(remote(pair.at[core], pair.at[core], pair_sem.at[0], pair_sem.at[1], sibling))
    swap.wait_recv()
    block = pair[...].reshape(2 * ROWS, KW)
    for h in range(2):
        quarters = [block[:, q * QUARTER : (q + 1) * QUARTER] for q in (h, 2 + h)]
        weight[2 * core + h, x, y, z] = jnp.where(core == 0, *quarters).astype(jnp.bfloat16)

    planes = [y, 1 - y]
    first, second = 2 * core, 2 * core + 1
    both = weight.at[pl.ds(first, 2), x, y, z]
    to_mirror = start(remote(both, both, y_sem.at[0], y_sem.at[1], mirror))

    def spread_x(index):
        own = weight.at[first, x, planes[index], z]
        return [
            start(remote(own, own, x_send.at[index, k], x_recv.at[index, k], others[k]))
            for k in range(NX - 1)
        ]

    x_copies = [spread_x(0), None]

    ring = {}

    def slot(h, index, by):
        if h == 0:
            return weight.at[first, :, planes[index], shift_z(by)]
        return weight.at[second, x, planes[index], shift_z(by)]

    WAYS = ((right, RIGHT, -1), (left, LEFT, 1))

    def ring_step(h, index, step):
        if step == 0:
            if index == 1 and h == 1:
                to_mirror.wait_recv()
                x_copies[1] = spread_x(1)
            if h == 0:
                for copy in x_copies[index]:
                    copy.wait_recv()
        for way, (device, steps, sign) in enumerate(WAYS):
            if 0 < step <= steps:
                ring[h, way, index, step - 1].wait_recv()
            if step < steps:
                ring[h, way, index, step] = start(
                    remote(
                        slot(h, index, sign * step),
                        slot(h, index, sign * step),
                        z_send.at[h, way, index, step],
                        z_recv.at[h, way, index, step],
                        device,
                    )
                )

    def arrived(step):
        return [
            (sign * step, step if way == 0 else RIGHT + step)
            for way, (_, steps, sign) in enumerate(WAYS)
            if step <= steps and (step > 0 or way == 0)
        ]

    shares, spread = [], {}

    def share(h, step):
        for by, order in arrived(step):
            if h == 1:
                for copy in spread[order]:
                    copy.wait_recv()
            both_planes = weight.at[2 * core + h, :, :, shift_z(by)]
            shares.append(
                start(
                    remote(both_planes, both_planes, share_send.at[h, order], share_recv.at[h, order], sibling)
                )
            )

    def spread_late(step):
        for by, order in arrived(step):
            mine = weight.at[second, x, :, shift_z(by)]
            spread[order] = [
                start(remote(mine, mine, late_send.at[order, k], late_recv.at[order, k], others[k]))
                for k in range(NX - 1)
            ]

    ring_step(1, 0, 0)

    load_grads.wait()
    grads_copies = [
        start(remote(grads, grads_in.at[x], grads_send.at[k], grads_recv.at[k], others[k]))
        for k in range(NX - 1)
    ]

    def normalise(c):
        rows = pl.ds(c * CHUNK, CHUNK)
        total = jnp.zeros((CHUNK, 1), jnp.float32)
        for j in range(NX):
            h = hid[rows, pl.ds(j * COLS, COLS)].astype(jnp.float32)
            total += jnp.sum(h * h, axis=-1, keepdims=True)
        scale = 1.0 / jnp.sqrt(total / D + 1e-05)
        scales[rows, :] = jnp.broadcast_to(scale, (CHUNK, 128))
        for j in range(NX):
            h = hid[rows, pl.ds(j * COLS, COLS)].astype(jnp.float32)
            normed = h * scale * gains[:, pl.ds(j * COLS, COLS)]
            normed_out[j, rows, :] = normed.astype(jnp.bfloat16)

    def spread_normed():
        copies = []
        for k in range(NX - 1):
            to = lax.rem(x + k + 1, NX)
            copies.append(
                start(
                    remote(normed_out.at[to], normed_in.at[x], normed_send.at[k], normed_recv.at[k], others[k])
                )
            )
        return copies

    load_hidden.wait()
    per_turn = CHUNKS // SEND_NORMED
    for turn in range(RIGHT + LAG + 3):
        if turn <= RIGHT:
            ring_step(0, 0, turn)
            if turn < RIGHT:
                ring_step(1, 0, turn + 1)
        if 0 <= turn - LAG <= RIGHT:
            ring_step(1, 1, turn - LAG)
            spread_late(turn - LAG)
            ring_step(0, 1, turn - LAG)
            share(0, turn - LAG)
        if 0 <= turn - LAG - 1 <= RIGHT:
            share(1, turn - LAG - 1)
        if turn < SEND_NORMED:
            for c in range(turn * per_turn, (turn + 1) * per_turn):
                normalise(c)
        if turn == SEND_NORMED:
            normed_copies = spread_normed()

    grads_in[x] = grads[...]
    normed_in[x] = normed_out[x]

    def part_tile(t):
        lhs = normed_in[:, :, pl.ds(t * TILE, TILE)].reshape(NX * TOK, TILE)
        product = lax.dot_general(
            lhs,
            grads_in[...].reshape(NX * TOK, KW),
            (((0,), (0,)), ((), ())),
            preferred_element_type=jnp.float32,
        )
        part[pl.ds(t * PAIRS, PAIRS)] = product.reshape(PAIRS, 2, ROWS, KW)
        return start(
            remote(
                part.at[pl.ds(t * PAIRS, PAIRS), 1 - core],
                part_in.at[pl.ds(t * PAIRS, PAIRS)],
                part_send.at[t],
                part_recv.at[t],
                sibling,
            )
        )

    halves = [1 - y, y]
    sums = {}

    def own_sum(half, by, piece):
        pair_index = halves[half] * NZ + shift_z(by)
        cols = pl.ds(piece * PIECE, PIECE)
        return part.at[pair_index, core, :, cols], part_in[pair_index, :, cols]

    def sum_step(step):
        for half in range(NY):
            for piece in range(PIECES):
                for way, (device, steps, sign) in enumerate(WAYS):
                    if step >= steps:
                        continue
                    mine, other = own_sum(half, sign * (step - steps), piece)
                    value = mine[...] + other
                    if step > 0:
                        sums[way, half, piece, step - 1].wait_recv()
                        value += land[way, step - 1, half, piece]
                    mine[...] = value
                    sums[way, half, piece, step] = start(
                        remote(
                            mine,
                            land.at[way, step, half, piece],
                            sum_send.at[way, step, half, piece],
                            sum_recv.at[way, step, half, piece],
                            device,
                        )
                    )

    for copy in shares:
        copy.wait_recv()

    @pl.loop(0, NX)
    def _(j):
        rows = jnp.concatenate([weight[q, j].reshape(COLS, QUARTER) for q in range(4)], axis=1)
        normed_grad[j] = lax.dot_general(
            grads[...], rows, (((1,), (1,)), ((), ())), preferred_element_type=jnp.float32
        )

    load_residual.wait()
    passes = []
    for c in range(CHUNKS):
        passes.append(
            remote(
                result.at[pl.ds(c * CHUNK, CHUNK)],
                passed.at[0, pl.ds(c * CHUNK, CHUNK)],
                pass_send.at[c],
                pass_recv.at[c],
                before,
            )
        )

    def input_grad(c):
        rows = pl.ds(c * CHUNK, CHUNK)
        scale = scales[rows, 0:1]
        total = jnp.zeros((CHUNK, 1), jnp.float32)
        for j in range(NX):
            cols = pl.ds(j * COLS, COLS)
            h = hid[rows, cols].astype(jnp.float32)
            weighted = normed_grad[j, rows, :] * gains[:, cols]
            total += jnp.sum(weighted * h, axis=-1, keepdims=True)
        factor = total / D * scale * scale * scale
        for j in range(NX):
            cols = pl.ds(j * COLS, COLS)
            h = hid[rows, cols].astype(jnp.float32)
            weighted = normed_grad[j, rows, :] * gains[:, cols]
            value = weighted * scale - h * factor + res[rows, cols].astype(jnp.float32)
            result[rows, cols] = value.astype(jnp.bfloat16)
        passes[c].start()

    @pl.when(s > 0)
    def _():
        for c in range(CHUNKS):
            input_grad(c)

    blanks = [
        pltpu.make_async_copy(zeros, passed.at[0, pl.ds(c * CHUNK, CHUNK)], pass_recv.at[c])
        for c in range(CHUNKS)
    ]

    @pl.when(s == NS - 1)
    def _():
        zeros[...] = jnp.zeros_like(zeros)
        for copy in blanks:
            copy.start()

    for copy in grads_copies + normed_copies:
        copy.wait_recv()
    part_copies = [part_tile(t) for t in range(TILES)]
    for copy in part_copies:
        copy.wait_recv()
    for step in range(RIGHT):
        sum_step(step)

    finals = []
    for half in range(NY):
        for piece in range(PIECES):
            mine, other = own_sum(half, 0, piece)
            value = mine[...] + other
            for way, (_, steps, _) in enumerate(WAYS):
                sums[way, half, piece, steps - 1].wait_recv()
                value += land[way, steps - 1, half, piece]
            if half == 0:
                mine[...] = value
                finals.append(
                    start(remote(mine, across.at[piece], across_send.at[piece], across_recv.at[piece], mirror))
                )
            else:
                finals[piece].wait_recv()
                grad_w[0, :, pl.ds(piece * PIECE, PIECE)] = (value + across[piece]) / math.sqrt(total_tokens)

    @pl.when(s < NS - 1)
    def _():
        for copy in passes:
            copy.wait_recv()

    @pl.when(s == NS - 1)
    def _():
        for copy in blanks:
            copy.wait()

    for copy in sent:
        copy.wait_send()

    @pl.when(s > 0)
    def _():
        for copy in passes:
            copy.wait_send()


def body(hidden, gain, key_grad, residual_grad, key_weight):
    total_tokens = hidden.shape[1] * lax.axis_size("fsdp")
    bf16, f32 = jnp.bfloat16, jnp.float32
    dma = pltpu.SemaphoreType.DMA
    return pl.pallas_call(
        functools.partial(kernel, total_tokens),
        out_shape=(
            jax.ShapeDtypeStruct((1, TOK, D), bf16),
            jax.ShapeDtypeStruct((1, ROWS, KW), f32),
        ),
        in_specs=[
            pl.BlockSpec(memory_space=pl.ANY),
            pl.BlockSpec(memory_space=pl.ANY),
            pl.BlockSpec(memory_space=pl.ANY),
            pl.BlockSpec(memory_space=pl.ANY),
            pl.BlockSpec(memory_space=pl.ANY),
        ],
        out_specs=(
            pl.BlockSpec(memory_space=pl.ANY),
            pl.BlockSpec(memory_space=pltpu.VMEM),
        ),
        scratch_shapes=[
            pltpu.VMEM((TOK, D), bf16),
            pltpu.VMEM((TOK, D), bf16),
            pltpu.VMEM((1, D), bf16),
            pltpu.VMEM((1, ROWS, KW), bf16),
            pltpu.VMEM((TOK, KW), bf16),
            pltpu.VMEM((1, D), f32),
            pltpu.VMEM((TOK, 128), f32),
            pltpu.VMEM((CHUNK, D), bf16),
            pltpu.VMEM((2, ROWS, KW), f32),
            pltpu.VMEM((4, NX, NY, NZ, 2 * ROWS, QUARTER), bf16),
            pltpu.VMEM((NX, TOK, COLS), bf16),
            pltpu.VMEM((NX, TOK, COLS), bf16),
            pltpu.VMEM((NX, TOK, KW), bf16),
            pltpu.VMEM((NY * NZ, 2, ROWS, KW), f32),
            pltpu.VMEM((NY * NZ, ROWS, KW), f32),
            pltpu.VMEM((2, RIGHT, NY, PIECES, ROWS, PIECE), f32),
            pltpu.VMEM((PIECES, ROWS, PIECE), f32),
            pltpu.VMEM((NX, TOK, COLS), f32),
            pltpu.VMEM((TOK, D), bf16),
            dma((5,)),
            dma((2,)),
            dma((2,)),
            dma((2, NX - 1)),
            dma((2, NX - 1)),
            dma((2, 2, 2, RIGHT)),
            dma((2, 2, 2, RIGHT)),
            dma((2, NZ)),
            dma((2, NZ)),
            dma((NZ, NX - 1)),
            dma((NZ, NX - 1)),
            dma((NX - 1,)),
            dma((NX - 1,)),
            dma((NX - 1,)),
            dma((NX - 1,)),
            dma((TILES,)),
            dma((TILES,)),
            dma((2, RIGHT, NY, PIECES)),
            dma((2, RIGHT, NY, PIECES)),
            dma((PIECES,)),
            dma((PIECES,)),
            dma((CHUNKS,)),
            dma((CHUNKS,)),
        ],
        compiler_params=pltpu.CompilerParams(
            collective_id=0, has_side_effects=True, vmem_limit_bytes=60 * 2**20
        ),
        cost_estimate=pl.CostEstimate(
            flops=4 * TOK * D * KW, bytes_accessed=16 * 2**20, transcendentals=TOK
        ),
        name="key_backward",
    )(hidden, gain, key_grad, residual_grad, key_weight)


def solution(mesh):
    return jax.shard_map(
        body,
        mesh=mesh,
        in_specs=(
            P("section", "fsdp", None),
            P("section", None),
            P("section", "fsdp", None),
            P("section", "fsdp", None),
            P("section", "fsdp", None),
        ),
        out_specs=(P("section", "fsdp", None), P("section", "fsdp", None)),
        check_vma=False,
    )
```

```python
import functools
import math

import jax
import jax.numpy as jnp
from jax import lax
from jax.experimental import pallas as pl
from jax.experimental.pallas import tpu as pltpu
from jax.sharding import PartitionSpec as P

MESH = pl.DeviceIdType.MESH
NX, NY, NZ, NS = 4, 2, 12, 4
RIGHT, LEFT = NZ // 2, (NZ - 1) // 2
TOK, KW, ROWS = 128, 512, 24
QUARTER = KW // 4
PIECES, PIECE = 2, KW // 2
COLS = NY * NZ * 2 * ROWS
D = NX * COLS
TILE = 384
TILES = COLS // TILE
PAIRS = TILE // (2 * ROWS)
CHUNK = 16
CHUNKS = TOK // CHUNK
LAG, LATE_LAG = 2, 1
PER_TURN = 1


def kernel(
    total_tokens,
    hidden,
    gain,
    key_grad,
    residual,
    key_weight,
    passed,
    grad_w,
    hid,
    res,
    gain_in,
    weight_in,
    grads,
    gains,
    scales,
    zeros,
    pair,
    weight,
    normed_out,
    normed_in,
    grads_in,
    part,
    part_in,
    land,
    across,
    normed_grad,
    result,
    load_sem,
    pair_sem,
    y_sem,
    x_send,
    x_recv,
    z_send,
    z_recv,
    share_send,
    share_recv,
    late_send,
    late_recv,
    grads_send,
    grads_recv,
    normed_send,
    normed_recv,
    part_send,
    part_recv,
    sum_send,
    sum_recv,
    across_send,
    across_recv,
    pass_send,
    pass_recv,
):
    s = lax.axis_index("section")
    f = lax.axis_index("fsdp")
    core = lax.rem(f, 2)
    z = lax.rem(f // 2, NZ)
    y = lax.rem(f // (2 * NZ), NY)
    x = f // (2 * NZ * NY)

    def at(x_, y_, z_, core_):
        return (s, ((x_ * NY + y_) * NZ + z_) * 2 + core_)

    def shift_z(by):
        return lax.rem(z + (by + 2 * NZ), NZ)

    sibling = at(x, y, z, 1 - core)
    mirror = at(x, 1 - y, z, core)
    right = at(x, y, shift_z(1), core)
    left = at(x, y, shift_z(-1), core)
    others = [at(lax.rem(x + k, NX), y, z, core) for k in range(1, NX)]
    before, after = (s - 1, f), (s + 1, f)

    def remote(src, dst, send, recv, device):
        copy = pltpu.make_async_remote_copy(
            src_ref=src,
            dst_ref=dst,
            send_sem=send,
            recv_sem=recv,
            device_id=device,
            device_id_type=MESH,
        )
        return copy

    load_hidden = pltpu.make_async_copy(hidden.at[0], hid, load_sem.at[0])
    load_grads = pltpu.make_async_copy(key_grad.at[0], grads, load_sem.at[1])
    load_residual = pltpu.make_async_copy(residual.at[0], res, load_sem.at[2])
    load_hidden.start()
    load_grads.start()
    load_residual.start()
    load_gain = pltpu.make_async_copy(gain, gain_in, load_sem.at[3])
    load_weight = pltpu.make_async_copy(key_weight, weight_in, load_sem.at[4])
    load_gain.start()
    load_weight.start()

    barrier = pltpu.get_barrier_semaphore()
    for device in [sibling, mirror, right, left] + others:
        pl.semaphore_signal(barrier, 1, device_id=device, device_id_type=MESH)

    @pl.when(s < NS - 1)
    def _():
        pl.semaphore_signal(barrier, 1, device_id=after, device_id_type=MESH)

    load_weight.wait()
    pair[core] = weight_in[0].astype(jnp.float32)
    load_gain.wait()
    gains[...] = gain_in[...].astype(jnp.float32)
    pl.semaphore_wait(barrier, 4 + len(others) + jnp.minimum(s, 1))

    sent = []

    def start(copy):
        copy.start()
        sent.append(copy)
        return copy

    swap = start(remote(pair.at[core], pair.at[core], pair_sem.at[0], pair_sem.at[1], sibling))
    swap.wait_recv()
    block = pair[...].reshape(2 * ROWS, KW)
    for h in range(2):
        quarters = [block[:, q * QUARTER : (q + 1) * QUARTER] for q in (h, 2 + h)]
        weight[2 * core + h, x, y, z] = jnp.where(core == 0, *quarters).astype(jnp.bfloat16)

    planes = [y, 1 - y]
    first, second = 2 * core, 2 * core + 1
    both = weight.at[pl.ds(first, 2), x, y, z]
    to_mirror = start(remote(both, both, y_sem.at[0], y_sem.at[1], mirror))

    def spread_x(index):
        own = weight.at[first, x, planes[index], z]
        return [
            start(remote(own, own, x_send.at[index, k], x_recv.at[index, k], others[k]))
            for k in range(NX - 1)
        ]

    x_copies = [spread_x(0), None]

    ring = {}

    def slot(h, index, by):
        if h == 0:
            return weight.at[first, :, planes[index], shift_z(by)]
        return weight.at[second, x, planes[index], shift_z(by)]

    WAYS = ((right, RIGHT, -1), (left, LEFT, 1))

    def ring_step(h, index, step):
        if step == 0:
            if index == 1 and h == 1:
                to_mirror.wait_recv()
                x_copies[1] = spread_x(1)
            if h == 0:
                for copy in x_copies[index]:
                    copy.wait_recv()
        for way, (device, steps, sign) in enumerate(WAYS):
            if 0 < step <= steps:
                ring[h, way, index, step - 1].wait_recv()
            if step < steps:
                ring[h, way, index, step] = start(
                    remote(
                        slot(h, index, sign * step),
                        slot(h, index, sign * step),
                        z_send.at[h, way, index, step],
                        z_recv.at[h, way, index, step],
                        device,
                    )
                )

    def arrived(step):
        return [
            (sign * step, step if way == 0 else RIGHT + step)
            for way, (_, steps, sign) in enumerate(WAYS)
            if step <= steps and (step > 0 or way == 0)
        ]

    shares, spread = [], {}

    def share(h, step):
        for by, order in arrived(step):
            if h == 1:
                for copy in spread[order]:
                    copy.wait_recv()
            both_planes = weight.at[2 * core + h, :, :, shift_z(by)]
            shares.append(
                start(
                    remote(both_planes, both_planes, share_send.at[h, order], share_recv.at[h, order], sibling)
                )
            )

    def spread_late(step):
        for by, order in arrived(step):
            mine = weight.at[second, x, :, shift_z(by)]
            spread[order] = [
                start(remote(mine, mine, late_send.at[order, k], late_recv.at[order, k], others[k]))
                for k in range(NX - 1)
            ]

    ring_step(1, 0, 0)

    load_grads.wait()
    grads_copies = [
        start(remote(grads, grads_in.at[x], grads_send.at[k], grads_recv.at[k], others[k]))
        for k in range(NX - 1)
    ]

    def normalise(c):
        rows = pl.ds(c * CHUNK, CHUNK)
        total = jnp.zeros((CHUNK, 1), jnp.float32)
        for j in range(NX):
            h = hid[rows, pl.ds(j * COLS, COLS)].astype(jnp.float32)
            total += jnp.sum(h * h, axis=-1, keepdims=True)
        scale = 1.0 / jnp.sqrt(total / D + 1e-05)
        scales[rows, :] = jnp.broadcast_to(scale, (CHUNK, 128))
        for j in range(NX):
            h = hid[rows, pl.ds(j * COLS, COLS)].astype(jnp.float32)
            normed = h * scale * gains[:, pl.ds(j * COLS, COLS)]
            normed_out[j, rows, :] = normed.astype(jnp.bfloat16)

    normed_copies = []

    def spread_normed(c):
        rows = pl.ds(c * CHUNK, CHUNK)
        for k in (0, 2, 1):
            to = lax.rem(x + k + 1, NX)
            normed_copies.append(
                start(
                    remote(
                        normed_out.at[to, rows],
                        normed_in.at[x, rows],
                        normed_send.at[c, k],
                        normed_recv.at[c, k],
                        others[k],
                    )
                )
            )

    load_hidden.wait()

    def part_tile(t):
        lhs = normed_in[:, :, pl.ds(t * TILE, TILE)].reshape(NX * TOK, TILE)
        product = lax.dot_general(
            lhs,
            grads_in[...].reshape(NX * TOK, KW),
            (((0,), (0,)), ((), ())),
            preferred_element_type=jnp.float32,
        )
        part[pl.ds(t * PAIRS, PAIRS)] = product.reshape(PAIRS, 2, ROWS, KW)
        return start(
            remote(
                part.at[pl.ds(t * PAIRS, PAIRS), 1 - core],
                part_in.at[pl.ds(t * PAIRS, PAIRS)],
                part_send.at[t],
                part_recv.at[t],
                sibling,
            )
        )

    for turn in range(RIGHT + LAG + 1):
        if turn <= RIGHT:
            ring_step(0, 0, turn)
            if turn < RIGHT:
                ring_step(1, 0, turn + 1)
        if 0 <= turn - LATE_LAG <= RIGHT:
            ring_step(1, 1, turn - LATE_LAG)
        if 0 <= turn - LAG <= RIGHT:
            ring_step(0, 1, turn - LAG)
        if 0 <= turn - LATE_LAG <= RIGHT:
            spread_late(turn - LATE_LAG)
        if 0 <= turn - LAG <= RIGHT:
            share(0, turn - LAG)
        if 0 <= turn - LATE_LAG - 1 <= RIGHT:
            share(1, turn - LATE_LAG - 1)
        for c in range(turn * PER_TURN, min((turn + 1) * PER_TURN, CHUNKS)):
            normalise(c)
            spread_normed(c)

    halves = [1 - y, y]
    sums = {}

    def own_sum(half, by, piece):
        pair_index = halves[half] * NZ + shift_z(by)
        cols = pl.ds(piece * PIECE, PIECE)
        return part.at[pair_index, core, :, cols], part_in[pair_index, :, cols]

    def sum_step(step):
        for half in range(NY):
            for piece in range(PIECES):
                for way, (device, steps, sign) in enumerate(WAYS):
                    if step >= steps:
                        continue
                    mine, other = own_sum(half, sign * (step - steps), piece)
                    value = mine[...] + other
                    if step > 0:
                        sums[way, half, piece, step - 1].wait_recv()
                        value += land[way, step - 1, half, piece]
                    mine[...] = value
                    sums[way, half, piece, step] = start(
                        remote(
                            mine,
                            land.at[way, step, half, piece],
                            sum_send.at[way, step, half, piece],
                            sum_recv.at[way, step, half, piece],
                            device,
                        )
                    )

    for copy in shares:
        copy.wait_recv()

    @pl.loop(0, NX)
    def _(j):
        rows = jnp.concatenate([weight[q, j].reshape(COLS, QUARTER) for q in range(4)], axis=1)
        normed_grad[j] = lax.dot_general(
            grads[...], rows, (((1,), (1,)), ((), ())), preferred_element_type=jnp.float32
        )

    load_residual.wait()
    passes = []
    for c in range(CHUNKS):
        passes.append(
            remote(
                result.at[pl.ds(c * CHUNK, CHUNK)],
                passed.at[0, pl.ds(c * CHUNK, CHUNK)],
                pass_send.at[c],
                pass_recv.at[c],
                before,
            )
        )

    def input_grad(c):
        rows = pl.ds(c * CHUNK, CHUNK)
        scale = scales[rows, 0:1]
        total = jnp.zeros((CHUNK, 1), jnp.float32)
        for j in range(NX):
            cols = pl.ds(j * COLS, COLS)
            h = hid[rows, cols].astype(jnp.float32)
            weighted = normed_grad[j, rows, :] * gains[:, cols]
            total += jnp.sum(weighted * h, axis=-1, keepdims=True)
        factor = total / D * scale * scale * scale
        for j in range(NX):
            cols = pl.ds(j * COLS, COLS)
            h = hid[rows, cols].astype(jnp.float32)
            weighted = normed_grad[j, rows, :] * gains[:, cols]
            value = weighted * scale - h * factor + res[rows, cols].astype(jnp.float32)
            result[rows, cols] = value.astype(jnp.bfloat16)
        passes[c].start()

    @pl.when(s > 0)
    def _():
        for c in range(CHUNKS):
            input_grad(c)

    blanks = [
        pltpu.make_async_copy(zeros, passed.at[0, pl.ds(c * CHUNK, CHUNK)], pass_recv.at[c])
        for c in range(CHUNKS)
    ]

    @pl.when(s == NS - 1)
    def _():
        zeros[...] = jnp.zeros_like(zeros)
        for copy in blanks:
            copy.start()

    grads_in[x] = grads[...]
    normed_in[x] = normed_out[x]
    for copy in grads_copies + normed_copies:
        copy.wait_recv()
    part_copies = [part_tile(t) for t in range(TILES)]
    for copy in part_copies:
        copy.wait_recv()
    for step in range(RIGHT):
        sum_step(step)

    finals = []
    for half in range(NY):
        for piece in range(PIECES):
            mine, other = own_sum(half, 0, piece)
            value = mine[...] + other
            for way, (_, steps, _) in enumerate(WAYS):
                sums[way, half, piece, steps - 1].wait_recv()
                value += land[way, steps - 1, half, piece]
            if half == 0:
                mine[...] = value
                finals.append(
                    start(remote(mine, across.at[piece], across_send.at[piece], across_recv.at[piece], mirror))
                )
            else:
                finals[piece].wait_recv()
                grad_w[0, :, pl.ds(piece * PIECE, PIECE)] = (value + across[piece]) / math.sqrt(total_tokens)

    @pl.when(s < NS - 1)
    def _():
        for copy in passes:
            copy.wait_recv()

    @pl.when(s == NS - 1)
    def _():
        for copy in blanks:
            copy.wait()

    for copy in sent:
        copy.wait_send()

    @pl.when(s > 0)
    def _():
        for copy in passes:
            copy.wait_send()


def body(hidden, gain, key_grad, residual_grad, key_weight):
    total_tokens = hidden.shape[1] * lax.axis_size("fsdp")
    bf16, f32 = jnp.bfloat16, jnp.float32
    dma = pltpu.SemaphoreType.DMA
    return pl.pallas_call(
        functools.partial(kernel, total_tokens),
        out_shape=(
            jax.ShapeDtypeStruct((1, TOK, D), bf16),
            jax.ShapeDtypeStruct((1, ROWS, KW), f32),
        ),
        in_specs=[
            pl.BlockSpec(memory_space=pl.ANY),
            pl.BlockSpec(memory_space=pl.ANY),
            pl.BlockSpec(memory_space=pl.ANY),
            pl.BlockSpec(memory_space=pl.ANY),
            pl.BlockSpec(memory_space=pl.ANY),
        ],
        out_specs=(
            pl.BlockSpec(memory_space=pl.ANY),
            pl.BlockSpec(memory_space=pltpu.VMEM),
        ),
        scratch_shapes=[
            pltpu.VMEM((TOK, D), bf16),
            pltpu.VMEM((TOK, D), bf16),
            pltpu.VMEM((1, D), bf16),
            pltpu.VMEM((1, ROWS, KW), bf16),
            pltpu.VMEM((TOK, KW), bf16),
            pltpu.VMEM((1, D), f32),
            pltpu.VMEM((TOK, 128), f32),
            pltpu.VMEM((CHUNK, D), bf16),
            pltpu.VMEM((2, ROWS, KW), f32),
            pltpu.VMEM((4, NX, NY, NZ, 2 * ROWS, QUARTER), bf16),
            pltpu.VMEM((NX, TOK, COLS), bf16),
            pltpu.VMEM((NX, TOK, COLS), bf16),
            pltpu.VMEM((NX, TOK, KW), bf16),
            pltpu.VMEM((NY * NZ, 2, ROWS, KW), f32),
            pltpu.VMEM((NY * NZ, ROWS, KW), f32),
            pltpu.VMEM((2, RIGHT, NY, PIECES, ROWS, PIECE), f32),
            pltpu.VMEM((PIECES, ROWS, PIECE), f32),
            pltpu.VMEM((NX, TOK, COLS), f32),
            pltpu.VMEM((TOK, D), bf16),
            dma((5,)),
            dma((2,)),
            dma((2,)),
            dma((2, NX - 1)),
            dma((2, NX - 1)),
            dma((2, 2, 2, RIGHT)),
            dma((2, 2, 2, RIGHT)),
            dma((2, NZ)),
            dma((2, NZ)),
            dma((NZ, NX - 1)),
            dma((NZ, NX - 1)),
            dma((NX - 1,)),
            dma((NX - 1,)),
            dma((CHUNKS, NX - 1)),
            dma((CHUNKS, NX - 1)),
            dma((TILES,)),
            dma((TILES,)),
            dma((2, RIGHT, NY, PIECES)),
            dma((2, RIGHT, NY, PIECES)),
            dma((PIECES,)),
            dma((PIECES,)),
            dma((CHUNKS,)),
            dma((CHUNKS,)),
        ],
        compiler_params=pltpu.CompilerParams(
            collective_id=0, has_side_effects=True, vmem_limit_bytes=60 * 2**20
        ),
        cost_estimate=pl.CostEstimate(
            flops=4 * TOK * D * KW, bytes_accessed=16 * 2**20, transcendentals=TOK
        ),
        name="key_backward",
    )(hidden, gain, key_grad, residual_grad, key_weight)


def solution(mesh):
    return jax.shard_map(
        body,
        mesh=mesh,
        in_specs=(
            P("section", "fsdp", None),
            P("section", None),
            P("section", "fsdp", None),
            P("section", "fsdp", None),
            P("section", "fsdp", None),
        ),
        out_specs=(P("section", "fsdp", None), P("section", "fsdp", None)),
        check_vma=False,
    )
```

```python
import functools
import math

import jax
import jax.numpy as jnp
from jax import lax
from jax.experimental import pallas as pl
from jax.experimental.pallas import tpu as pltpu
from jax.sharding import PartitionSpec as P

MESH = pl.DeviceIdType.MESH
NX, NY, NZ, NS = 4, 2, 12, 4
RIGHT, LEFT = NZ // 2, (NZ - 1) // 2
TOK, KW, ROWS = 128, 512, 24
QUARTER = KW // 4
PIECES, PIECE = 2, KW // 2
COLS = NY * NZ * 2 * ROWS
D = NX * COLS
TILE = 384
TILES = COLS // TILE
PAIRS = TILE // (2 * ROWS)
CHUNK = 16
CHUNKS = TOK // CHUNK
LAG, LATE_LAG = 2, 1
PER_TURN = 1


def kernel(
    total_tokens,
    hidden,
    gain,
    key_grad,
    residual,
    key_weight,
    passed,
    grad_w,
    hid,
    res,
    gain_in,
    weight_in,
    grads,
    gains,
    scales,
    zeros,
    pair,
    weight,
    normed_out,
    normed_in,
    grads_in,
    part,
    part_in,
    land,
    across,
    normed_grad,
    result,
    load_sem,
    pair_sem,
    y_sem,
    x_send,
    x_recv,
    z_send,
    z_recv,
    share_send,
    share_recv,
    late_send,
    late_recv,
    grads_send,
    grads_recv,
    normed_send,
    normed_recv,
    part_send,
    part_recv,
    sum_send,
    sum_recv,
    across_send,
    across_recv,
    pass_send,
    pass_recv,
):
    s = lax.axis_index("section")
    f = lax.axis_index("fsdp")
    core = lax.rem(f, 2)
    z = lax.rem(f // 2, NZ)
    y = lax.rem(f // (2 * NZ), NY)
    x = f // (2 * NZ * NY)

    def at(x_, y_, z_, core_):
        return (s, ((x_ * NY + y_) * NZ + z_) * 2 + core_)

    def shift_z(by):
        return lax.rem(z + (by + 2 * NZ), NZ)

    sibling = at(x, y, z, 1 - core)
    mirror = at(x, 1 - y, z, core)
    right = at(x, y, shift_z(1), core)
    left = at(x, y, shift_z(-1), core)
    others = [at(lax.rem(x + k, NX), y, z, core) for k in range(1, NX)]
    before, after = (s - 1, f), (s + 1, f)

    def remote(src, dst, send, recv, device):
        copy = pltpu.make_async_remote_copy(
            src_ref=src,
            dst_ref=dst,
            send_sem=send,
            recv_sem=recv,
            device_id=device,
            device_id_type=MESH,
        )
        return copy

    load_hidden = pltpu.make_async_copy(hidden.at[0], hid, load_sem.at[0])
    load_grads = pltpu.make_async_copy(key_grad.at[0], grads, load_sem.at[1])
    load_residual = pltpu.make_async_copy(residual.at[0], res, load_sem.at[2])
    load_hidden.start()
    load_grads.start()
    load_residual.start()
    load_gain = pltpu.make_async_copy(gain, gain_in, load_sem.at[3])
    load_weight = pltpu.make_async_copy(key_weight, weight_in, load_sem.at[4])
    load_gain.start()
    load_weight.start()

    barrier = pltpu.get_barrier_semaphore()
    for device in [sibling, mirror, right, left] + others:
        pl.semaphore_signal(barrier, 1, device_id=device, device_id_type=MESH)

    @pl.when(s < NS - 1)
    def _():
        pl.semaphore_signal(barrier, 1, device_id=after, device_id_type=MESH)

    load_weight.wait()
    pair[core] = weight_in[0].astype(jnp.float32)
    load_gain.wait()
    gains[...] = gain_in[...].astype(jnp.float32)
    pl.semaphore_wait(barrier, 4 + len(others) + jnp.minimum(s, 1))

    sent = []

    def start(copy):
        copy.start()
        sent.append(copy)
        return copy

    swap = start(remote(pair.at[core], pair.at[core], pair_sem.at[0], pair_sem.at[1], sibling))
    swap.wait_recv()
    block = pair[...].reshape(2 * ROWS, KW)
    for h in range(2):
        quarters = [block[:, q * QUARTER : (q + 1) * QUARTER] for q in (h, 2 + h)]
        weight[2 * core + h, x, y, z] = jnp.where(core == 0, *quarters).astype(jnp.bfloat16)

    planes = [y, 1 - y]
    first, second = 2 * core, 2 * core + 1
    both = weight.at[pl.ds(first, 2), x, y, z]
    to_mirror = start(remote(both, both, y_sem.at[0], y_sem.at[1], mirror))

    def spread_x(index):
        own = weight.at[first, x, planes[index], z]
        return [
            start(remote(own, own, x_send.at[index, k], x_recv.at[index, k], others[k]))
            for k in range(NX - 1)
        ]

    x_copies = [spread_x(0), None]

    ring = {}

    def slot(h, index, by):
        if h == 0:
            return weight.at[first, :, planes[index], shift_z(by)]
        return weight.at[second, x, planes[index], shift_z(by)]

    WAYS = ((right, RIGHT, -1), (left, LEFT, 1))

    def ring_step(h, index, step):
        if step == 0:
            if index == 1 and h == 1:
                to_mirror.wait_recv()
                x_copies[1] = spread_x(1)
            if h == 0:
                for copy in x_copies[index]:
                    copy.wait_recv()
        for way, (device, steps, sign) in enumerate(WAYS):
            if 0 < step <= steps:
                ring[h, way, index, step - 1].wait_recv()
            if step < steps:
                ring[h, way, index, step] = start(
                    remote(
                        slot(h, index, sign * step),
                        slot(h, index, sign * step),
                        z_send.at[h, way, index, step],
                        z_recv.at[h, way, index, step],
                        device,
                    )
                )

    def arrived(step):
        return [
            (sign * step, step if way == 0 else RIGHT + step)
            for way, (_, steps, sign) in enumerate(WAYS)
            if step <= steps and (step > 0 or way == 0)
        ]

    shares, spread = [], {}

    def share(h, step):
        for by, order in arrived(step):
            if h == 1:
                for copy in spread[order]:
                    copy.wait_recv()
            both_planes = weight.at[2 * core + h, :, :, shift_z(by)]
            shares.append(
                start(
                    remote(both_planes, both_planes, share_send.at[h, order], share_recv.at[h, order], sibling)
                )
            )

    def spread_late(step):
        for by, order in arrived(step):
            mine = weight.at[second, x, :, shift_z(by)]
            spread[order] = [
                start(remote(mine, mine, late_send.at[order, k], late_recv.at[order, k], others[k]))
                for k in range(NX - 1)
            ]

    ring_step(1, 0, 0)

    load_grads.wait()
    grads_copies = []

    def normalise(c):
        rows = pl.ds(c * CHUNK, CHUNK)
        total = jnp.zeros((CHUNK, 1), jnp.float32)
        for j in range(NX):
            h = hid[rows, pl.ds(j * COLS, COLS)].astype(jnp.float32)
            total += jnp.sum(h * h, axis=-1, keepdims=True)
        scale = 1.0 / jnp.sqrt(total / D + 1e-05)
        scales[rows, :] = jnp.broadcast_to(scale, (CHUNK, 128))
        for j in range(NX):
            h = hid[rows, pl.ds(j * COLS, COLS)].astype(jnp.float32)
            normed = h * scale * gains[:, pl.ds(j * COLS, COLS)]
            normed_out[j, rows, :] = normed.astype(jnp.bfloat16)

    normed_copies = []

    def spread_normed(c):
        rows = pl.ds(c * CHUNK, CHUNK)
        for k in (0, 2, 1):
            to = lax.rem(x + k + 1, NX)
            normed_copies.append(
                start(
                    remote(
                        normed_out.at[to, rows],
                        normed_in.at[x, rows],
                        normed_send.at[c, k],
                        normed_recv.at[c, k],
                        others[k],
                    )
                )
            )

    load_hidden.wait()

    def part_tile(t):
        lhs = normed_in[:, :, pl.ds(t * TILE, TILE)].reshape(NX * TOK, TILE)
        product = lax.dot_general(
            lhs,
            grads_in[...].reshape(NX * TOK, KW),
            (((0,), (0,)), ((), ())),
            preferred_element_type=jnp.float32,
        )
        part[pl.ds(t * PAIRS, PAIRS)] = product.reshape(PAIRS, 2, ROWS, KW)
        return start(
            remote(
                part.at[pl.ds(t * PAIRS, PAIRS), 1 - core],
                part_in.at[pl.ds(t * PAIRS, PAIRS)],
                part_send.at[t],
                part_recv.at[t],
                sibling,
            )
        )

    for turn in range(RIGHT + LAG + 1):
        if turn <= RIGHT:
            ring_step(0, 0, turn)
            if turn < RIGHT:
                ring_step(1, 0, turn + 1)
        if 0 <= turn - LATE_LAG <= RIGHT:
            ring_step(1, 1, turn - LATE_LAG)
        if 0 <= turn - LAG <= RIGHT:
            ring_step(0, 1, turn - LAG)
        if 0 <= turn - LATE_LAG <= RIGHT:
            spread_late(turn - LATE_LAG)
        if 0 <= turn - LAG <= RIGHT:
            share(0, turn - LAG)
        if 0 <= turn - LATE_LAG - 1 <= RIGHT:
            share(1, turn - LATE_LAG - 1)
        if 0 < turn < NX:
            k = turn - 1
            grads_copies.append(
                start(remote(grads, grads_in.at[x], grads_send.at[k], grads_recv.at[k], others[k]))
            )
        for c in range(turn * PER_TURN, min((turn + 1) * PER_TURN, CHUNKS)):
            normalise(c)
            spread_normed(c)

    halves = [1 - y, y]
    sums = {}

    def own_sum(half, by, piece):
        pair_index = halves[half] * NZ + shift_z(by)
        cols = pl.ds(piece * PIECE, PIECE)
        return part.at[pair_index, core, :, cols], part_in[pair_index, :, cols]

    def sum_step(step):
        for half in range(NY):
            for piece in range(PIECES):
                for way, (device, steps, sign) in enumerate(WAYS):
                    if step >= steps:
                        continue
                    mine, other = own_sum(half, sign * (step - steps), piece)
                    value = mine[...] + other
                    if step > 0:
                        sums[way, half, piece, step - 1].wait_recv()
                        value += land[way, step - 1, half, piece]
                    mine[...] = value
                    sums[way, half, piece, step] = start(
                        remote(
                            mine,
                            land.at[way, step, half, piece],
                            sum_send.at[way, step, half, piece],
                            sum_recv.at[way, step, half, piece],
                            device,
                        )
                    )

    for copy in shares:
        copy.wait_recv()

    @pl.loop(0, NX)
    def _(j):
        rows = jnp.concatenate([weight[q, j].reshape(COLS, QUARTER) for q in range(4)], axis=1)
        normed_grad[j] = lax.dot_general(
            grads[...], rows, (((1,), (1,)), ((), ())), preferred_element_type=jnp.float32
        )

    load_residual.wait()
    passes = []
    for c in range(CHUNKS):
        passes.append(
            remote(
                result.at[pl.ds(c * CHUNK, CHUNK)],
                passed.at[0, pl.ds(c * CHUNK, CHUNK)],
                pass_send.at[c],
                pass_recv.at[c],
                before,
            )
        )

    def input_grad(c):
        rows = pl.ds(c * CHUNK, CHUNK)
        scale = scales[rows, 0:1]
        total = jnp.zeros((CHUNK, 1), jnp.float32)
        for j in range(NX):
            cols = pl.ds(j * COLS, COLS)
            h = hid[rows, cols].astype(jnp.float32)
            weighted = normed_grad[j, rows, :] * gains[:, cols]
            total += jnp.sum(weighted * h, axis=-1, keepdims=True)
        factor = total / D * scale * scale * scale
        for j in range(NX):
            cols = pl.ds(j * COLS, COLS)
            h = hid[rows, cols].astype(jnp.float32)
            weighted = normed_grad[j, rows, :] * gains[:, cols]
            value = weighted * scale - h * factor + res[rows, cols].astype(jnp.float32)
            result[rows, cols] = value.astype(jnp.bfloat16)
        passes[c].start()

    @pl.when(s > 0)
    def _():
        for c in range(CHUNKS):
            input_grad(c)

    blanks = [
        pltpu.make_async_copy(zeros, passed.at[0, pl.ds(c * CHUNK, CHUNK)], pass_recv.at[c])
        for c in range(CHUNKS)
    ]

    @pl.when(s == NS - 1)
    def _():
        zeros[...] = jnp.zeros_like(zeros)
        for copy in blanks:
            copy.start()

    grads_in[x] = grads[...]
    normed_in[x] = normed_out[x]
    for copy in grads_copies + normed_copies:
        copy.wait_recv()
    part_copies = [part_tile(t) for t in range(TILES)]
    for copy in part_copies:
        copy.wait_recv()
    for step in range(RIGHT):
        sum_step(step)

    finals = []
    for half in range(NY):
        for piece in range(PIECES):
            mine, other = own_sum(half, 0, piece)
            value = mine[...] + other
            for way, (_, steps, _) in enumerate(WAYS):
                sums[way, half, piece, steps - 1].wait_recv()
                value += land[way, steps - 1, half, piece]
            if half == 0:
                mine[...] = value
                finals.append(
                    start(remote(mine, across.at[piece], across_send.at[piece], across_recv.at[piece], mirror))
                )
            else:
                finals[piece].wait_recv()
                grad_w[0, :, pl.ds(piece * PIECE, PIECE)] = (value + across[piece]) / math.sqrt(total_tokens)

    @pl.when(s < NS - 1)
    def _():
        for copy in passes:
            copy.wait_recv()

    @pl.when(s == NS - 1)
    def _():
        for copy in blanks:
            copy.wait()

    for copy in sent:
        copy.wait_send()

    @pl.when(s > 0)
    def _():
        for copy in passes:
            copy.wait_send()


def body(hidden, gain, key_grad, residual_grad, key_weight):
    total_tokens = hidden.shape[1] * lax.axis_size("fsdp")
    bf16, f32 = jnp.bfloat16, jnp.float32
    dma = pltpu.SemaphoreType.DMA
    return pl.pallas_call(
        functools.partial(kernel, total_tokens),
        out_shape=(
            jax.ShapeDtypeStruct((1, TOK, D), bf16),
            jax.ShapeDtypeStruct((1, ROWS, KW), f32),
        ),
        in_specs=[
            pl.BlockSpec(memory_space=pl.ANY),
            pl.BlockSpec(memory_space=pl.ANY),
            pl.BlockSpec(memory_space=pl.ANY),
            pl.BlockSpec(memory_space=pl.ANY),
            pl.BlockSpec(memory_space=pl.ANY),
        ],
        out_specs=(
            pl.BlockSpec(memory_space=pl.ANY),
            pl.BlockSpec(memory_space=pltpu.VMEM),
        ),
        scratch_shapes=[
            pltpu.VMEM((TOK, D), bf16),
            pltpu.VMEM((TOK, D), bf16),
            pltpu.VMEM((1, D), bf16),
            pltpu.VMEM((1, ROWS, KW), bf16),
            pltpu.VMEM((TOK, KW), bf16),
            pltpu.VMEM((1, D), f32),
            pltpu.VMEM((TOK, 128), f32),
            pltpu.VMEM((CHUNK, D), bf16),
            pltpu.VMEM((2, ROWS, KW), f32),
            pltpu.VMEM((4, NX, NY, NZ, 2 * ROWS, QUARTER), bf16),
            pltpu.VMEM((NX, TOK, COLS), bf16),
            pltpu.VMEM((NX, TOK, COLS), bf16),
            pltpu.VMEM((NX, TOK, KW), bf16),
            pltpu.VMEM((NY * NZ, 2, ROWS, KW), f32),
            pltpu.VMEM((NY * NZ, ROWS, KW), f32),
            pltpu.VMEM((2, RIGHT, NY, PIECES, ROWS, PIECE), f32),
            pltpu.VMEM((PIECES, ROWS, PIECE), f32),
            pltpu.VMEM((NX, TOK, COLS), f32),
            pltpu.VMEM((TOK, D), bf16),
            dma((5,)),
            dma((2,)),
            dma((2,)),
            dma((2, NX - 1)),
            dma((2, NX - 1)),
            dma((2, 2, 2, RIGHT)),
            dma((2, 2, 2, RIGHT)),
            dma((2, NZ)),
            dma((2, NZ)),
            dma((NZ, NX - 1)),
            dma((NZ, NX - 1)),
            dma((NX - 1,)),
            dma((NX - 1,)),
            dma((CHUNKS, NX - 1)),
            dma((CHUNKS, NX - 1)),
            dma((TILES,)),
            dma((TILES,)),
            dma((2, RIGHT, NY, PIECES)),
            dma((2, RIGHT, NY, PIECES)),
            dma((PIECES,)),
            dma((PIECES,)),
            dma((CHUNKS,)),
            dma((CHUNKS,)),
        ],
        compiler_params=pltpu.CompilerParams(
            collective_id=0, has_side_effects=True, vmem_limit_bytes=60 * 2**20
        ),
        cost_estimate=pl.CostEstimate(
            flops=4 * TOK * D * KW, bytes_accessed=16 * 2**20, transcendentals=TOK
        ),
        name="key_backward",
    )(hidden, gain, key_grad, residual_grad, key_weight)


def solution(mesh):
    return jax.shard_map(
        body,
        mesh=mesh,
        in_specs=(
            P("section", "fsdp", None),
            P("section", None),
            P("section", "fsdp", None),
            P("section", "fsdp", None),
            P("section", "fsdp", None),
        ),
        out_specs=(P("section", "fsdp", None), P("section", "fsdp", None)),
        check_vma=False,
    )
```
